512 devices in a mesh: avg: 16 (over x, y_lo, core), space: 32 (over z, y_hi).
Axes of the slice: x: 4, y: 4 (y_hi: 2, y_lo: 2; y = y_hi * 2 + y_lo), z: 16, core: 2. Of those that a mesh axis runs over, the one named last changes fastest.
Arguments:
- spectral_state: float32 [3, 2, 1024, 1024], P(None, None, 'space', 'avg'), may hold values from -6 to 6
- phase_index: int32 [16], P('avg'), may hold values from 0 to 63
- weight_count: int32 [16], P('avg'), may hold values from 1 to 7
Outputs:
- advanced: float32 [3, 2, 1024, 1024], P(None, None, 'space', 'avg')
The draws below stay inside these ranges and needn't reach their ends.
All inputs are finite; a program needn't handle non-finite values.
Results may differ from the reference program's by a relative error of at most 0.015.
Values may be sent and summed in bfloat16 or wider, within the bound.
No kernel may reach another device: no remote copies, remote signals or barrier semaphores. Data moves between devices by JAX's collectives and lax.ppermute only.
A program may use at most 64 MiB of HBM per device.

```python
import jax
import jax.numpy as jnp
from jax import lax

N = 1024
PHASES = 16


def set_ends(drawn, rng, low, largest):
    shape = drawn.shape
    spot = [jax.random.randint(jax.random.fold_in(rng, axis), (), 0, shape[axis]) for axis in range(len(shape))]
    drawn = drawn.at[tuple(spot)].set(low)
    longest = shape.index(max(shape))
    spot[longest] = (spot[longest] + 1) % shape[longest]
    return drawn.at[tuple(spot)].set(largest)


def levels(own_key, dims, shards, low, high):
    factor_of, own = 1.0, jax.random.fold_in(own_key, 6)
    for position, shards_of in shards:
        steps = jnp.exp(jax.random.uniform(jax.random.fold_in(own, position), (shards_of,), jnp.float32, low / len(shards), high / len(shards)))
        factor_of = factor_of * jnp.repeat(steps, dims[position] // shards_of).reshape([-1 if axis == position else 1 for axis in range(len(dims))])
    return factor_of


def scatter_about(own_key, shape, deviation, reach, cuts=(), kind=jnp.bfloat16):
    gain = levels(own_key, shape, cuts, -0.22, 0.18) if cuts else 1.0
    drawn = jax.random.normal(own_key, shape, jnp.float32) * deviation * gain
    return jnp.minimum(jnp.maximum(drawn, -reach), reach).astype(kind)


def setup_inputs(seed: int = 0) -> dict:
    splits = jax.random.split(jax.random.key(seed), 4)
    return {
        "spectral_state": scatter_about(splits[0], (3, 2, N, N), 1.0, 6.0, ((2, 32), (3, 16)), jnp.float32),
        "phase_index": set_ends(jax.random.randint(splits[1], (PHASES,), 0, 64), jax.random.fold_in(splits[1], 1), 0, 63).astype(jnp.int32),
        "weight_count": set_ends(jax.random.randint(splits[2], (PHASES,), 1, 8), jax.random.fold_in(splits[2], 1), 1, 7).astype(jnp.int32),
    }


coriolis = 1.0
wave_speed = 6.0
phase_step = 0.25
time_step = 2.0
weight_scale = 4.0

def wavenumbers(length):
    positions = jnp.arange(length, dtype=jnp.int32)
    shifted = (positions + length // 2) % length - length // 2
    return shifted.astype(jnp.float32) * (2.0 / length)

def wave_operator(fields, wave_rows, wave_columns):
    east_real, north_real, height_real = (fields[0, 0], fields[1, 0], fields[2, 0])
    east_imag, north_imag, height_imag = (fields[0, 1], fields[1, 1], fields[2, 1])
    real_part = jnp.stack([coriolis * north_real + wave_speed * wave_rows * height_imag, -coriolis * east_real + wave_speed * wave_columns * height_imag, wave_speed * (wave_rows * east_imag + wave_columns * north_imag)])
    imag_part = jnp.stack([coriolis * north_imag - wave_speed * wave_rows * height_real, -coriolis * east_imag - wave_speed * wave_columns * height_real, -wave_speed * (wave_rows * east_real + wave_columns * north_real)])
    return jnp.stack([real_part, imag_part], axis=1)

def wave_exponential(fields, wave_rows, wave_columns, phase_value):
    frequency = jnp.sqrt(coriolis * coriolis + wave_speed * wave_speed * (wave_rows * wave_rows + wave_columns * wave_columns))
    sine_term = jnp.sin(frequency * phase_value) / frequency
    cosine_term = (1.0 - jnp.cos(frequency * phase_value)) / (frequency * frequency)
    single = wave_operator(fields, wave_rows, wave_columns)
    double = wave_operator(single, wave_rows, wave_columns)
    return fields + sine_term * single + cosine_term * double

def flux_tendency(spectra, wave_rows, wave_columns):
    real_part, imag_part = (spectra[:, 0], spectra[:, 1])

    def divergence(planes):
        flux_east = jnp.stack([planes[0], planes[1], planes[3]])
        flux_north = jnp.stack([planes[1], planes[2], planes[4]])
        return wave_rows * flux_east + wave_columns * flux_north
    return jnp.stack([divergence(imag_part), -divergence(real_part)], axis=1)

def rounded(values):
    return lax.optimization_barrier(values.astype(jnp.bfloat16)).astype(jnp.float32)

def rounded_complex(values):
    return lax.complex(rounded(values.real), rounded(values.imag))

def reference(spectral_state, phase_index, weight_count):
    wave_table = wavenumbers(N)
    wave_rows = wave_table[:, None]
    wave_columns = wave_table[None, :]
    total_phases = phase_index.shape[0]

    def one_phase(running_sum, inputs):
        sample_index, numerator = inputs
        phase_value = sample_index.astype(jnp.float32) * phase_step
        weight_value = numerator.astype(jnp.float32) / (weight_scale * total_phases)
        rotated = rounded(wave_exponential(spectral_state, wave_rows, wave_columns, phase_value))
        spectral = lax.complex(rotated[:, 0], rotated[:, 1])
        half_done = rounded_complex(jnp.fft.ifft(spectral, axis=2) * N)
        physical = jnp.fft.ifft(half_done, axis=1).real
        east_wind, north_wind, height = (physical[0], physical[1], physical[2])
        products = rounded(jnp.stack([east_wind * east_wind, east_wind * north_wind, north_wind * north_wind, east_wind * height, north_wind * height]))
        forward_half = rounded_complex(jnp.fft.fft(products, axis=1))
        spectra = jnp.fft.fft(forward_half, axis=2) / N
        stacked = jnp.stack([spectra.real, spectra.imag], axis=1)
        tendency = flux_tendency(stacked, wave_rows, wave_columns)
        rotated_back = wave_exponential(tendency, wave_rows, wave_columns, -phase_value)
        return (running_sum + weight_value * rotated_back, None)
    running_sum, unused = lax.scan(one_phase, jnp.zeros(spectral_state.shape, jnp.float32), (phase_index, weight_count))
    return wave_exponential(spectral_state + time_step * running_sum, wave_rows, wave_columns, time_step)
```

```python
import math

import jax
import jax.numpy as jnp
import numpy as np
from jax import lax
from jax.experimental import pallas as pl
from jax.experimental.pallas import tpu as pltpu
from jax.sharding import PartitionSpec as P

N = 1024
LANES = 128
ROWS = 32
HALF = 16

coriolis = 1.0
wave_speed = 6.0
phase_step = 0.25
time_step = 2.0
weight_scale = 64.0

VMEM_LIMIT = 28 * 1024 * 1024
F32 = jnp.float32
BF16 = jnp.bfloat16


def fourier_tables():
    positions = np.arange(N, dtype=np.int64)
    angles = (positions[:, None] * positions[None, :] % N).astype(np.float64) * (2.0 * math.pi / N)
    return jnp.asarray(np.cos(angles), BF16), jnp.asarray(np.sin(angles), BF16)


def wave_of(index):
    shifted = jnp.where(index >= N // 2, index - N, index)
    return shifted.astype(F32) * (2.0 / N)


def sine_cosine(angle):
    turns = jnp.floor(angle * (2.0 / math.pi) + 0.5)
    rest = angle - turns * 1.5703125
    rest = rest - turns * 4.837512969970703125e-4
    rest = rest - turns * 7.54978995489188216e-8
    square = rest * rest
    sine = ((-1.9515295891e-4 * square + 8.3321608736e-3) * square - 1.6666654611e-1) * square * rest + rest
    cosine = ((2.443315711809948e-5 * square - 1.388731625493765e-3) * square + 4.166664568298827e-2) * square * square
    cosine = cosine - 0.5 * square + 1.0
    quarter = turns.astype(jnp.int32)
    odd = (quarter & 1) == 1
    sine_out = jnp.where(odd, cosine, sine)
    cosine_out = jnp.where(odd, sine, cosine)
    sine_out = jnp.where((quarter & 2) == 2, -sine_out, sine_out)
    cosine_out = jnp.where(((quarter + 1) & 2) == 2, -cosine_out, cosine_out)
    return sine_out, cosine_out


def exponential_terms(wave_rows, wave_columns, phase_value):
    squared = coriolis * coriolis + (wave_speed * wave_speed) * (
        wave_rows * wave_rows + wave_columns * wave_columns
    )
    inverse = lax.rsqrt(squared)
    inverse = inverse * (1.5 - 0.5 * squared * inverse * inverse)
    sine, cosine = sine_cosine(squared * inverse * phase_value)
    return sine * inverse, (1.0 - cosine) * (inverse * inverse)


def wave_operator(fields, speed_rows, speed_columns):
    east_r, east_i, north_r, north_i, height_r, height_i = fields
    return (
        coriolis * north_r + speed_rows * height_i,
        coriolis * north_i - speed_rows * height_r,
        speed_columns * height_i - coriolis * east_r,
        -speed_columns * height_r - coriolis * east_i,
        speed_rows * east_i + speed_columns * north_i,
        -(speed_rows * east_r + speed_columns * north_r),
    )


def wave_exponential(fields, wave_rows, wave_columns, sine_term, cosine_term):
    speed_rows = wave_speed * wave_rows
    speed_columns = wave_speed * wave_columns
    single = wave_operator(fields, speed_rows, speed_columns)
    double = wave_operator(single, speed_rows, speed_columns)
    return [w + sine_term * a + cosine_term * b for w, a, b in zip(fields, single, double)]


def lanes_of(rows):
    return lax.broadcasted_iota(jnp.int32, (rows, LANES), 1)


def swap_halves(even, odd):
    low = lanes_of(even.shape[0]) < 64
    return (
        jnp.where(low, even, pltpu.roll(odd, 64, 1)),
        jnp.where(low, pltpu.roll(even, 64, 1), odd),
    )


def swap_quarters(parts):
    lane = lanes_of(parts[0].shape[0])
    odd = (lane & 32) == 32
    first, second, third, fourth = parts
    first, second = (
        jnp.where(odd, pltpu.roll(second, 32, 1), first),
        jnp.where(odd, second, pltpu.roll(first, 96, 1)),
    )
    third, fourth = (
        jnp.where(odd, pltpu.roll(fourth, 32, 1), third),
        jnp.where(odd, fourth, pltpu.roll(third, 96, 1)),
    )
    first, third = swap_halves(first, third)
    second, fourth = swap_halves(second, fourth)
    return first, second, third, fourth


def spread_kernel(state_ref, out_ref):
    for plane in range(6):
        low = state_ref[plane // 2, plane % 2, :HALF, :]
        high = state_ref[plane // 2, plane % 2, HALF:, :]
        packed = jnp.concatenate([low, high], axis=1).astype(BF16)
        for target in range(16):
            out_ref[target, HALF * plane : HALF * (plane + 1), :] = packed


def first_kernel(phase_ref, gathered_ref, cosine_ref, sine_ref, out_ref, rotated):
    phase_value = phase_ref[0].astype(F32) * phase_step
    row_start = lax.axis_index("space") * ROWS
    for group in range(8):
        planes = []
        for plane in range(6):
            rows = slice(HALF * plane, HALF * (plane + 1))
            planes.append(
                swap_halves(
                    gathered_ref[2 * group, rows, :].astype(F32),
                    gathered_ref[2 * group + 1, rows, :].astype(F32),
                )
            )
        wave_columns = wave_of(lanes_of(HALF) + LANES * group)
        for half in range(2):
            row = lax.broadcasted_iota(jnp.int32, (HALF, LANES), 0) + (row_start + HALF * half)
            wave_rows = wave_of(row)
            terms = exponential_terms(wave_rows, wave_columns, phase_value)
            result = wave_exponential([p[half] for p in planes], wave_rows, wave_columns, *terms)
            for plane in range(6):
                start = ROWS * plane + HALF * half
                rotated[start : start + HALF, LANES * group : LANES * (group + 1)] = result[
                    plane
                ].astype(BF16)
    for chunk in range(4):
        columns = slice(256 * chunk, 256 * (chunk + 1))
        data = rotated[...]
        cosine = jnp.dot(data, cosine_ref[:, columns], preferred_element_type=F32)
        sine = jnp.dot(data, sine_ref[:, columns], preferred_element_type=F32)
        for part in range(2):
            lanes = slice(LANES * part, LANES * (part + 1))
            real, imag = [], []
            for field in range(3):
                top = slice(64 * field, 64 * field + ROWS)
                bottom = slice(64 * field + ROWS, 64 * (field + 1))
                real.append(cosine[top, lanes] - sine[bottom, lanes])
                imag.append(sine[top, lanes] + cosine[bottom, lanes])
            main = swap_quarters([real[0], real[1], real[2], imag[0]])
            extra = swap_quarters(
                [imag[1][:HALF], imag[2][:HALF], imag[1][HALF:], imag[2][HALF:]]
            )
            for offset in range(4):
                target = 8 * chunk + 4 * part + offset
                out_ref[target, :ROWS, :] = main[offset].astype(BF16)
                out_ref[target, ROWS:, :] = extra[offset].astype(BF16)


def second_kernel(arrived_ref, cosine_ref, sine_ref, out_ref, real_part, imag_part, pairs):
    lane = lanes_of(HALF)
    first = lane < 32
    for source in range(32):
        for half in range(2):
            rows = slice(HALF * half, HALF * (half + 1))
            main = arrived_ref[source, rows, :]
            target = slice(ROWS * source + HALF * half, ROWS * source + HALF * (half + 1))
            real_part[target, :] = main
            rest = arrived_ref[source, ROWS:, :].astype(F32)
            rest = pltpu.roll(rest, 96 if half else 32, 1)
            imag = jnp.where(first, pltpu.roll(main.astype(F32), 32, 1), rest)
            imag_part[target, :] = (-imag).astype(BF16)
    lane = lanes_of(256)
    quarter = lane // 32
    for chunk in range(4):
        rows = slice(256 * chunk, 256 * (chunk + 1))
        grid = jnp.dot(cosine_ref[rows, :], real_part[...], preferred_element_type=F32)
        grid = grid + jnp.dot(sine_ref[rows, :], imag_part[...], preferred_element_type=F32)
        grid = grid * (1.0 / N)
        up = pltpu.roll(grid, 32, 1)
        down = pltpu.roll(grid, 96, 1)
        left = jnp.where(quarter == 0, grid, jnp.where(quarter == 3, down, up))
        right = jnp.where(quarter < 2, grid, up)
        pairs[rows, :LANES] = (left * right).astype(BF16)
        pairs[rows, LANES:] = (grid * down).astype(BF16)
    lane = lanes_of(HALF)
    quarter = lane // 32
    for chunk in range(4):
        rows = slice(256 * chunk, 256 * (chunk + 1))
        real = jnp.dot(cosine_ref[rows, :], pairs[...], preferred_element_type=F32)
        imag = -jnp.dot(sine_ref[rows, :], pairs[...], preferred_element_type=F32)
        for offset in range(8):
            target = 8 * chunk + offset
            top = slice(ROWS * offset, ROWS * offset + HALF)
            bottom = slice(ROWS * offset + HALF, ROWS * (offset + 1))
            both = slice(ROWS * offset, ROWS * (offset + 1))
            out_ref[target, :ROWS, :] = real[both, :LANES].astype(BF16)
            out_ref[target, ROWS : 2 * ROWS, :] = imag[both, :LANES].astype(BF16)
            extra = jnp.where(
                quarter < 2,
                jnp.where(quarter == 0, pltpu.roll(real[top, LANES:], 96, 1), real[bottom, LANES:]),
                jnp.where(
                    quarter == 2,
                    pltpu.roll(imag[top, LANES:], 32, 1),
                    pltpu.roll(imag[bottom, LANES:], 64, 1),
                ),
            )
            out_ref[target, 2 * ROWS :, :] = extra.astype(BF16)


def third_kernel(phase_ref, weight_ref, returned_ref, cosine_ref, sine_ref, out_ref, lines):
    phase_value = phase_ref[0].astype(F32) * phase_step
    weight = weight_ref[0].astype(F32) * (1.0 / weight_scale)
    row_start = lax.axis_index("space") * ROWS
    for group in range(8):
        columns = slice(LANES * group, LANES * (group + 1))
        for part in range(2):
            rows = slice(ROWS * part, ROWS * (part + 1))
            blocks = swap_quarters(
                [returned_ref[4 * group + offset, rows, :].astype(F32) for offset in range(4)]
            )
            for product in range(4):
                start = 160 * part + ROWS * product
                lines[start : start + ROWS, columns] = blocks[product].astype(BF16)
        blocks = swap_quarters(
            [returned_ref[4 * group + offset, 2 * ROWS :, :].astype(F32) for offset in range(4)]
        )
        for index in range(4):
            start = 160 * (index // 2) + 128 + HALF * (index % 2)
            lines[start : start + HALF, columns] = blocks[index].astype(BF16)
    for chunk in range(4):
        columns = slice(256 * chunk, 256 * (chunk + 1))
        data = lines[...]
        cosine = jnp.dot(data, cosine_ref[:, columns], preferred_element_type=F32)
        sine = jnp.dot(data, sine_ref[:, columns], preferred_element_type=F32)
        for part in range(2):
            lanes = slice(LANES * part, LANES * (part + 1))
            group = 2 * chunk + part
            wave_columns = wave_of(lanes_of(HALF) + LANES * group)
            halves = []
            for half in range(2):
                row = lax.broadcasted_iota(jnp.int32, (HALF, LANES), 0) + (row_start + HALF * half)
                wave_rows = wave_of(row)
                real, imag = [], []
                for product in range(5):
                    start = ROWS * product + HALF * half
                    top = slice(start, start + HALF)
                    bottom = slice(160 + start, 160 + start + HALF)
                    real.append((cosine[top, lanes] + sine[bottom, lanes]) * (1.0 / N))
                    imag.append((cosine[bottom, lanes] - sine[top, lanes]) * (1.0 / N))
                tendency = []
                for toward_east, toward_north in ((0, 1), (1, 2), (3, 4)):
                    tendency.append(wave_rows * imag[toward_east] + wave_columns * imag[toward_north])
                    tendency.append(
                        -(wave_rows * real[toward_east] + wave_columns * real[toward_north])
                    )
                sine_term, cosine_term = exponential_terms(wave_rows, wave_columns, phase_value)
                result = wave_exponential(
                    tendency, wave_rows, wave_columns, -sine_term, cosine_term
                )
                halves.append([weight * plane for plane in result])
            for plane in range(6):
                even, odd = swap_halves(halves[0][plane], halves[1][plane])
                rows = slice(HALF * plane, HALF * (plane + 1))
                out_ref[2 * group, rows, :] = even.astype(BF16)
                out_ref[2 * group + 1, rows, :] = odd.astype(BF16)


def last_kernel(state_ref, parts_ref, out_ref):
    lane = lanes_of(HALF)
    high = lane >= 64
    column = (lane & 63) + lax.axis_index("avg") * 64
    row = lax.broadcasted_iota(jnp.int32, (HALF, LANES), 0) + lax.axis_index("space") * ROWS
    wave_rows = wave_of(jnp.where(high, row + HALF, row))
    wave_columns = wave_of(column)
    fields = []
    for plane in range(6):
        rows = slice(HALF * plane, HALF * (plane + 1))
        total = parts_ref[0, rows, :].astype(F32)
        for source in range(1, 16):
            total = total + parts_ref[source, rows, :].astype(F32)
        low_rows = state_ref[plane // 2, plane % 2, :HALF, :]
        high_rows = state_ref[plane // 2, plane % 2, HALF:, :]
        fields.append(jnp.concatenate([low_rows, high_rows], axis=1) + time_step * total)
    terms = exponential_terms(wave_rows, wave_columns, time_step)
    result = wave_exponential(fields, wave_rows, wave_columns, *terms)
    for plane in range(6):
        out_ref[plane // 2, plane % 2, :HALF, :] = result[plane][:, :64]
        out_ref[plane // 2, plane % 2, HALF:, :] = result[plane][:, 64:]


def call(kernel, name, shape, dtype, scratch, places):
    spots = [pl.BlockSpec(memory_space=pltpu.SMEM if p == "s" else pltpu.VMEM) for p in places]
    return pl.pallas_call(
        kernel,
        name=name,
        out_shape=jax.ShapeDtypeStruct(shape, dtype),
        in_specs=spots,
        out_specs=pl.BlockSpec(memory_space=pltpu.VMEM),
        scratch_shapes=[pltpu.VMEM(s, BF16) for s in scratch],
        compiler_params=pltpu.CompilerParams(vmem_limit_bytes=VMEM_LIMIT),
    )


def per_device(spectral_state, phase_index, weight_count):
    cosine_table, sine_table = fourier_tables()
    spread = call(spread_kernel, "spread", (16, 96, LANES), BF16, [], "v")(spectral_state)
    gathered = lax.all_to_all(spread, "avg", 0, 0)
    outgoing = call(first_kernel, "inverse_columns", (32, 48, LANES), BF16, [(192, N)], "svvv")(
        phase_index, gathered, cosine_table, sine_table
    )
    arrived = lax.all_to_all(outgoing, "space", 0, 0)
    outgoing_back = call(
        second_kernel,
        "grid_products",
        (32, 80, LANES),
        BF16,
        [(N, LANES), (N, LANES), (N, 2 * LANES)],
        "vvv",
    )(arrived, cosine_table, sine_table)
    returned = lax.all_to_all(outgoing_back, "space", 0, 0)
    weighted = call(third_kernel, "forward_columns", (16, 96, LANES), BF16, [(320, N)], "ssvvv")(
        phase_index, weight_count, returned, cosine_table, sine_table
    )
    parts = lax.all_to_all(weighted, "avg", 0, 0)
    return call(last_kernel, "advance", spectral_state.shape, F32, [], "vv")(spectral_state, parts)


def solution(mesh):
    in_specs = (P(None, None, "space", "avg"), P("avg"), P("avg"))
    out_specs = P(None, None, "space", "avg")
    return jax.shard_map(
        per_device, mesh=mesh, in_specs=in_specs, out_specs=out_specs, check_vma=False
    )
```

```python
import math

import jax
import jax.numpy as jnp
import numpy as np
from jax import lax
from jax.experimental import pallas as pl
from jax.experimental.pallas import tpu as pltpu
from jax.sharding import Mesh
from jax.sharding import PartitionSpec as P

N = 1024
LANES = 128
ROWS = 32
LINES = 16

coriolis = 1.0
wave_speed = 6.0
phase_step = 0.25
time_step = 2.0
weight_scale = 64.0

VMEM_LIMIT = 28 * 1024 * 1024
F32 = jnp.float32
BF16 = jnp.bfloat16
MAIN_AXES = ("zb", "zm", "yh")
GROUP_AXES = ("xy", "c", "zm", "yh")


def fourier_tables():
    positions = np.arange(N, dtype=np.int64)
    angles = (positions[:, None] * positions[None, :] % N).astype(np.float64) * (2.0 * math.pi / N)
    return jnp.asarray(np.stack([np.cos(angles), np.sin(angles)]), BF16)


def wave_of(index):
    shifted = jnp.where(index >= N // 2, index - N, index)
    return shifted.astype(F32) * (2.0 / N)


def sine_cosine(angle):
    turns = jnp.floor(angle * (2.0 / math.pi) + 0.5)
    rest = angle - turns * 1.5703125
    rest = rest - turns * 4.837512969970703125e-4
    rest = rest - turns * 7.54978995489188216e-8
    square = rest * rest
    sine = ((-1.9515295891e-4 * square + 8.3321608736e-3) * square - 1.6666654611e-1) * square * rest + rest
    cosine = ((2.443315711809948e-5 * square - 1.388731625493765e-3) * square + 4.166664568298827e-2) * square * square
    cosine = cosine - 0.5 * square + 1.0
    quarter = turns.astype(jnp.int32)
    odd = (quarter & 1) == 1
    sine_out = jnp.where(odd, cosine, sine)
    cosine_out = jnp.where(odd, sine, cosine)
    sine_out = jnp.where((quarter & 2) == 2, -sine_out, sine_out)
    cosine_out = jnp.where(((quarter + 1) & 2) == 2, -cosine_out, cosine_out)
    return sine_out, cosine_out


def exponential_terms(wave_rows, wave_columns, phase_value):
    squared = coriolis * coriolis + (wave_speed * wave_speed) * (
        wave_rows * wave_rows + wave_columns * wave_columns
    )
    inverse = lax.rsqrt(squared)
    inverse = inverse * (1.5 - 0.5 * squared * inverse * inverse)
    sine, cosine = sine_cosine(squared * inverse * phase_value)
    return sine * inverse, (1.0 - cosine) * (inverse * inverse)


def wave_operator(fields, speed_rows, speed_columns):
    east_r, east_i, north_r, north_i, height_r, height_i = fields
    return (
        coriolis * north_r + speed_rows * height_i,
        coriolis * north_i - speed_rows * height_r,
        speed_columns * height_i - coriolis * east_r,
        -speed_columns * height_r - coriolis * east_i,
        speed_rows * east_i + speed_columns * north_i,
        -(speed_rows * east_r + speed_columns * north_r),
    )


def wave_exponential(fields, wave_rows, wave_columns, sine_term, cosine_term):
    speed_rows = wave_speed * wave_rows
    speed_columns = wave_speed * wave_columns
    single = wave_operator(fields, speed_rows, speed_columns)
    double = wave_operator(single, speed_rows, speed_columns)
    return [w + sine_term * a + cosine_term * b for w, a, b in zip(fields, single, double)]


def lanes_of(rows):
    return lax.broadcasted_iota(jnp.int32, (rows, LANES), 1)


def roll(values, shift):
    return pltpu.roll(values, shift % LANES, 1)


def swap_blocks(parts, width):
    parts = list(parts)
    lane = lanes_of(parts[0].shape[0])
    step = 1
    while step < len(parts):
        shift = width * step
        odd = (lane & shift) == shift
        for low in range(len(parts)):
            if low & step:
                continue
            high = low | step
            parts[low], parts[high] = (
                jnp.where(odd, roll(parts[high], shift), parts[low]),
                jnp.where(odd, parts[high], roll(parts[low], -shift)),
            )
        step *= 2
    return parts


def own_columns(rows):
    device = (lax.axis_index("xy") * 2 + lax.axis_index("c")) * 4
    device = device + lax.axis_index("zm") * 2 + lax.axis_index("yh")
    return wave_of(lax.broadcasted_iota(jnp.int32, (rows, LANES), 0) + device * LINES)


def spread_kernel(state_ref, out_ref):
    def plane(index):
        return state_ref[index // 2, index % 2]

    left = jnp.concatenate([plane(index) for index in range(4)], axis=0)
    right = jnp.concatenate([plane(4), plane(5), jnp.zeros((64, 64), F32)], axis=0)
    turned = jnp.concatenate([left, right], axis=1).T
    low = lanes_of(8) < 64
    for part in range(4):
        main = turned[LINES * part : LINES * (part + 1)]
        rest = turned[64 + LINES * part : 64 + LINES * (part + 1)]
        rest = jnp.where(low, rest[:8], roll(rest[8:], 64))
        message = jnp.concatenate([main, rest], axis=0).astype(BF16)
        for block in range(8):
            out_ref[4 * block + part] = message


def first_kernel(settings_ref, gathered_ref, table_ref, out_ref, rotated):
    wave_columns = own_columns(LINES)
    for group in range(8):
        lanes = slice(LANES * group, LANES * (group + 1))
        messages = [gathered_ref[4 * group + offset].astype(F32) for offset in range(4)]
        planes = swap_blocks([message[:16] for message in messages], 32)
        rest = swap_blocks([message[16:] for message in messages], 32)
        planes.append(jnp.concatenate([rest[0], rest[2]], axis=0))
        planes.append(jnp.concatenate([rest[1], rest[3]], axis=0))
        wave_rows = wave_of(lanes_of(LINES) + LANES * group)
        for phase in range(2):
            phase_value = settings_ref[phase, 0].astype(F32) * phase_step
            terms = exponential_terms(wave_rows, wave_columns, phase_value)
            result = wave_exponential(planes, wave_rows, wave_columns, *terms)
            for plane in range(6):
                start = 96 * phase + LINES * plane
                rotated[start : start + LINES, lanes] = result[plane].astype(BF16)
    for chunk in range(4):
        columns = slice(256 * chunk, 256 * (chunk + 1))
        data = rotated[...]
        cosine = jnp.dot(data, table_ref[0, :, columns], preferred_element_type=F32)
        sine = jnp.dot(data, table_ref[1, :, columns], preferred_element_type=F32)
        for part in range(2):
            lanes = slice(LANES * part, LANES * (part + 1))
            real, imag = [], []
            for field in range(6):
                top = slice(32 * field, 32 * field + LINES)
                bottom = slice(32 * field + LINES, 32 * (field + 1))
                real.append(cosine[top, lanes] - sine[bottom, lanes])
                imag.append(sine[top, lanes] + cosine[bottom, lanes])
            main = swap_blocks(real + imag[:2], 16)
            rest = swap_blocks([v[:8] for v in imag[2:]] + [v[8:] for v in imag[2:]], 16)
            for offset in range(8):
                message = jnp.concatenate([main[offset], rest[offset]], axis=0)
                out_ref[8 * (2 * chunk + part) + offset] = message.astype(BF16)


def second_kernel(arrived_ref, table_ref, out_ref, real_part, imag_part, pairs):
    first = lanes_of(LINES) < 32
    for source in range(64):
        message = arrived_ref[source].astype(F32)
        main, rest = message[:16], message[16:]
        rest = jnp.concatenate([roll(rest, 32), roll(rest, -32)], axis=0)
        imag = jnp.where(first, roll(main, 32), rest)
        rows = slice(LINES * source, LINES * (source + 1))
        real_part[rows, :] = main.astype(BF16)
        imag_part[rows, :] = (-imag).astype(BF16)
    block = lanes_of(256) // 16
    height_lanes = (block == 2) | (block == 5)
    for chunk in range(4):
        rows = slice(256 * chunk, 256 * (chunk + 1))
        grid = jnp.dot(table_ref[0, rows, :], real_part[...], preferred_element_type=F32)
        grid = grid + jnp.dot(table_ref[1, rows, :], imag_part[...], preferred_element_type=F32)
        grid = grid * (1.0 / N)
        other = jnp.where(height_lanes, roll(grid, 32), grid)
        pairs[rows, :LANES] = (grid * other).astype(BF16)
        pairs[rows, LANES:] = (grid * roll(grid, 16)).astype(BF16)
    lane = lanes_of(LINES)
    short = lanes_of(8)
    for chunk in range(4):
        rows = slice(256 * chunk, 256 * (chunk + 1))
        real = jnp.dot(table_ref[0, rows, :], pairs[...], preferred_element_type=F32)
        imag = -jnp.dot(table_ref[1, rows, :], pairs[...], preferred_element_type=F32)
        for offset in range(16):
            own = slice(LINES * offset, LINES * (offset + 1))
            real_rest, imag_rest = real[own, LANES:], imag[own, LANES:]
            first_rows = jnp.where(lane < 96, real[own, :LANES], roll(real_rest, 80))
            second_rows = jnp.where(lane < 96, imag[own, :LANES], roll(imag_rest, 80))
            last_rows = jnp.where(
                short < 64,
                jnp.where(short < 32, roll(real_rest[:8], 64), roll(imag_rest[:8], -32)),
                jnp.where(short < 96, real_rest[8:], roll(imag_rest[8:], 32)),
            )
            message = jnp.concatenate([first_rows, second_rows, last_rows], axis=0)
            out_ref[16 * chunk + offset] = message.astype(BF16)


PRODUCT_ORDER = ((0, 0), (0, 2), (0, 3), (1, 0), (1, 2), (1, 3), (0, 1), (0, 4))


def third_kernel(settings_ref, returned_ref, table_ref, out_ref, lines):
    wave_columns = own_columns(LINES)
    for group in range(8):
        lanes = slice(LANES * group, LANES * (group + 1))
        messages = [returned_ref[8 * group + offset].astype(F32) for offset in range(8)]
        rest = swap_blocks([message[32:] for message in messages], 16)
        for part in range(2):
            blocks = swap_blocks([m[16 * part : 16 * (part + 1)] for m in messages], 16)
            places = list(PRODUCT_ORDER) + [(1, 1), (1, 4)]
            blocks.append(jnp.concatenate([rest[2 * part], rest[4 + 2 * part]], axis=0))
            blocks.append(jnp.concatenate([rest[2 * part + 1], rest[5 + 2 * part]], axis=0))
            for (phase, product), block in zip(places, blocks):
                start = 160 * part + 80 * phase + LINES * product
                lines[start : start + LINES, lanes] = block.astype(BF16)
    for chunk in range(4):
        columns = slice(256 * chunk, 256 * (chunk + 1))
        data = lines[...]
        cosine = jnp.dot(data, table_ref[0, :, columns], preferred_element_type=F32)
        sine = jnp.dot(data, table_ref[1, :, columns], preferred_element_type=F32)
        for part in range(2):
            lanes = slice(LANES * part, LANES * (part + 1))
            group = 2 * chunk + part
            wave_rows = wave_of(lanes_of(LINES) + LANES * group)
            total = None
            for phase in range(2):
                phase_value = settings_ref[phase, 0].astype(F32) * phase_step
                weight = settings_ref[phase, 1].astype(F32) * (1.0 / weight_scale)
                real, imag = [], []
                for product in range(5):
                    start = 80 * phase + LINES * product
                    top = slice(start, start + LINES)
                    bottom = slice(160 + start, 160 + start + LINES)
                    real.append((cosine[top, lanes] + sine[bottom, lanes]) * (1.0 / N))
                    imag.append((cosine[bottom, lanes] - sine[top, lanes]) * (1.0 / N))
                tendency = []
                for toward_east, toward_north in ((0, 1), (1, 2), (3, 4)):
                    tendency.append(wave_rows * imag[toward_east] + wave_columns * imag[toward_north])
                    tendency.append(
                        -(wave_rows * real[toward_east] + wave_columns * real[toward_north])
                    )
                sine_term, cosine_term = exponential_terms(wave_rows, wave_columns, phase_value)
                result = wave_exponential(
                    tendency, wave_rows, wave_columns, -sine_term, cosine_term
                )
                result = [weight * plane for plane in result]
                total = result if total is None else [a + b for a, b in zip(total, result)]
            main = swap_blocks(total[:4], 32)
            rest = swap_blocks([total[4][:8], total[5][:8], total[4][8:], total[5][8:]], 32)
            for offset in range(4):
                message = jnp.concatenate([main[offset], rest[offset]], axis=0)
                out_ref[4 * group + offset] = message.astype(BF16)


def last_kernel(state_ref, parts_ref, out_ref):
    mains, rests = [], []
    for part in range(4):
        total = parts_ref[part].astype(F32)
        for block in range(1, 8):
            total = total + parts_ref[4 * block + part].astype(F32)
        mains.append(total[:16])
        rests.append(jnp.concatenate([total[16:], roll(total[16:], 64)], axis=0))
    turned = jnp.concatenate(mains + rests, axis=0).T
    row_start = (lax.axis_index("zb") * 4 + lax.axis_index("zm") * 2 + lax.axis_index("yh")) * ROWS
    column_start = (lax.axis_index("xy") * 2 + lax.axis_index("c")) * 64
    wave_rows = wave_of(lax.broadcasted_iota(jnp.int32, (ROWS, 64), 0) + row_start)
    wave_columns = wave_of(lax.broadcasted_iota(jnp.int32, (ROWS, 64), 1) + column_start)
    fields = []
    for plane in range(6):
        rows = slice(ROWS * (plane % 4), ROWS * (plane % 4 + 1))
        total = turned[rows, :64] if plane < 4 else turned[rows, 64:]
        fields.append(state_ref[plane // 2, plane % 2] + time_step * total)
    terms = exponential_terms(wave_rows, wave_columns, time_step)
    result = wave_exponential(fields, wave_rows, wave_columns, *terms)
    for plane in range(6):
        out_ref[plane // 2, plane % 2] = result[plane]


def call(kernel, name, shape, dtype, scratch, places, flops):
    spots = [pl.BlockSpec(memory_space=pltpu.SMEM if p == "s" else pltpu.VMEM) for p in places]
    return pl.pallas_call(
        kernel,
        name=name,
        out_shape=jax.ShapeDtypeStruct(shape, dtype),
        in_specs=spots,
        out_specs=pl.BlockSpec(memory_space=pltpu.VMEM),
        scratch_shapes=[pltpu.VMEM(s, BF16) for s in scratch],
        cost_estimate=pl.CostEstimate(flops=flops, bytes_accessed=1 << 20, transcendentals=0),
        compiler_params=pltpu.CompilerParams(vmem_limit_bytes=VMEM_LIMIT),
    )


def per_device(spectral_state, phase_index, weight_count):
    tables = fourier_tables()
    settings = lax.all_gather(jnp.stack([phase_index, weight_count], axis=1), "c", axis=0, tiled=True)
    settings = lax.ppermute(
        settings, ("xy", "zb"), [(8 * i + j, 8 * j + i) for i in range(8) for j in range(8)]
    )
    spread = call(spread_kernel, "spread", (32, 24, LANES), BF16, [], "v", 1 << 33)(spectral_state)
    gathered = lax.all_to_all(spread, MAIN_AXES, 0, 0)
    outgoing = call(first_kernel, "inverse_rows", (64, 24, LANES), BF16, [(192, N)], "svv", 1 << 30)(
        settings, gathered, tables
    )
    arrived = lax.all_to_all(outgoing, GROUP_AXES, 0, 0)
    outgoing_back = call(
        second_kernel,
        "grid_products",
        (64, 40, LANES),
        BF16,
        [(N, LANES), (N, LANES), (N, 2 * LANES)],
        "vv",
        1 << 30,
    )(arrived, tables)
    returned = lax.all_to_all(outgoing_back, GROUP_AXES, 0, 0)
    weighted = call(third_kernel, "forward_rows", (32, 24, LANES), BF16, [(320, N)], "svv", 1 << 31)(
        settings, returned, tables
    )
    parts = lax.all_to_all(weighted, MAIN_AXES, 0, 0)
    return call(last_kernel, "advance", spectral_state.shape, F32, [], "vv", 1 << 24)(spectral_state, parts)


def solution(mesh):
    fine = Mesh(mesh.devices.reshape(8, 2, 8, 2, 2), ("xy", "c", "zb", "zm", "yh"))
    rows, columns = ("zb", "zm", "yh"), ("xy", "c")
    in_specs = (P(None, None, rows, columns), P(columns), P(columns))
    out_specs = P(None, None, rows, columns)
    return jax.shard_map(
        per_device, mesh=fine, in_specs=in_specs, out_specs=out_specs, check_vma=False
    )
```

```python
import math

import jax
import jax.numpy as jnp
import numpy as np
from jax import lax
from jax.experimental import pallas as pl
from jax.experimental.pallas import tpu as pltpu
from jax.sharding import Mesh
from jax.sharding import PartitionSpec as P

N = 1024
LANES = 128
ROWS = 32
LINES = 16

coriolis = 1.0
wave_speed = 6.0
phase_step = 0.25
time_step = 2.0
weight_scale = 64.0

VMEM_LIMIT = 28 * 1024 * 1024
F32 = jnp.float32
BF16 = jnp.bfloat16
MAIN_AXES = ("zl", "zm", "zh", "yh")
GROUP_AXES = ("xy", "c", "zm", "yh")


def fourier_tables():
    product = np.arange(N)[:, None] * np.arange(N // 2)[None, :] % N
    angles = product.astype(np.float64) * (2.0 * math.pi / N)
    tables = np.stack([np.cos(angles), np.sin(angles)])
    return jnp.asarray(tables, BF16), jnp.asarray(tables.transpose(0, 2, 1), BF16)


def wave_of(index):
    shifted = jnp.where(index >= N // 2, index - N, index)
    return shifted.astype(F32) * (2.0 / N)


def sine_cosine(angle):
    turns = jnp.floor(angle * (2.0 / math.pi) + 0.5)
    rest = angle - turns * 1.5703125
    rest = rest - turns * 4.837512969970703125e-4
    rest = rest - turns * 7.54978995489188216e-8
    square = rest * rest
    sine = ((-1.9515295891e-4 * square + 8.3321608736e-3) * square - 1.6666654611e-1) * square * rest + rest
    cosine = ((2.443315711809948e-5 * square - 1.388731625493765e-3) * square + 4.166664568298827e-2) * square * square
    cosine = cosine - 0.5 * square + 1.0
    quarter = turns.astype(jnp.int32)
    odd = (quarter & 1) == 1
    sine_out = jnp.where(odd, cosine, sine)
    cosine_out = jnp.where(odd, sine, cosine)
    sine_out = jnp.where((quarter & 2) == 2, -sine_out, sine_out)
    cosine_out = jnp.where(((quarter + 1) & 2) == 2, -cosine_out, cosine_out)
    return sine_out, cosine_out


def exponential_terms(wave_rows, wave_columns, phase_value):
    squared = coriolis * coriolis + (wave_speed * wave_speed) * (
        wave_rows * wave_rows + wave_columns * wave_columns
    )
    inverse = lax.rsqrt(squared)
    inverse = inverse * (1.5 - 0.5 * squared * inverse * inverse)
    sine, cosine = sine_cosine(squared * inverse * phase_value)
    return sine * inverse, (1.0 - cosine) * (inverse * inverse)


def wave_operator(fields, speed_rows, speed_columns):
    east_r, east_i, north_r, north_i, height_r, height_i = fields
    return (
        coriolis * north_r + speed_rows * height_i,
        coriolis * north_i - speed_rows * height_r,
        speed_columns * height_i - coriolis * east_r,
        -speed_columns * height_r - coriolis * east_i,
        speed_rows * east_i + speed_columns * north_i,
        -(speed_rows * east_r + speed_columns * north_r),
    )


def wave_exponential(fields, wave_rows, wave_columns, sine_term, cosine_term):
    speed_rows = wave_speed * wave_rows
    speed_columns = wave_speed * wave_columns
    single = wave_operator(fields, speed_rows, speed_columns)
    double = wave_operator(single, speed_rows, speed_columns)
    return [w + sine_term * a + cosine_term * b for w, a, b in zip(fields, single, double)]


def lanes_of(rows):
    return lax.broadcasted_iota(jnp.int32, (rows, LANES), 1)


def roll(values, shift):
    return pltpu.roll(values, shift % LANES, 1)


def swap_blocks(parts, width):
    parts = list(parts)
    lane = lanes_of(parts[0].shape[0])
    step = 1
    while step < len(parts):
        shift = width * step
        odd = (lane & shift) == shift
        for low in range(len(parts)):
            if low & step:
                continue
            high = low | step
            parts[low], parts[high] = (
                jnp.where(odd, roll(parts[high], shift), parts[low]),
                jnp.where(odd, parts[high], roll(parts[low], -shift)),
            )
        step *= 2
    return parts


def slot(device):
    high, low, rest = device // 16, device // 4 % 4, device % 4
    return low * 8 + rest // 2 * 4 + high * 2 + rest % 2


def own_block():
    return 4 * lax.axis_index("zh") + lax.axis_index("zl")


def alternate(values, axis):
    index = lax.broadcasted_iota(jnp.int32, values.shape, axis)
    return jnp.where((index & 1) == 1, -values, values)


def own_columns(rows):
    device = (lax.axis_index("xy") * 2 + lax.axis_index("c")) * 4
    device = device + lax.axis_index("zm") * 2 + lax.axis_index("yh")
    return wave_of(lax.broadcasted_iota(jnp.int32, (rows, LANES), 0) + device * LINES)


def spread_kernel(phase_ref, weight_ref, state_ref, out_ref, settings_ref):
    phase_value = phase_ref[0].astype(F32) * phase_step
    weight = weight_ref[0].astype(F32) * (1.0 / weight_scale)
    settings_ref[...] = jnp.where(lanes_of(8) < 64, phase_value, weight)

    def plane(index):
        return state_ref[index // 2, index % 2]

    left = jnp.concatenate([plane(index) for index in range(4)], axis=0)
    right = jnp.concatenate([plane(4), plane(5), jnp.zeros((64, 64), F32)], axis=0)
    turned = jnp.concatenate([left, right], axis=1).T
    low = lanes_of(8) < 64
    for part in range(4):
        main = turned[LINES * part : LINES * (part + 1)]
        rest = turned[64 + LINES * part : 64 + LINES * (part + 1)]
        rest = jnp.where(low, rest[:8], roll(rest[8:], 64))
        message = jnp.concatenate([main, rest], axis=0).astype(BF16)
        for block in range(8):
            out_ref[slot(4 * block + part)] = message


def first_kernel(settings_ref, gathered_ref, table_ref, out_ref, rotated):
    wave_columns = own_columns(LINES)
    for group in range(8):
        lanes = slice(LANES * group, LANES * (group + 1))
        messages = [gathered_ref[slot(4 * group + offset)].astype(F32) for offset in range(4)]
        planes = swap_blocks([message[:16] for message in messages], 32)
        rest = swap_blocks([message[16:] for message in messages], 32)
        planes.append(jnp.concatenate([rest[0], rest[2]], axis=0))
        planes.append(jnp.concatenate([rest[1], rest[3]], axis=0))
        wave_rows = wave_of(lanes_of(LINES) + LANES * group)
        for phase in range(2):
            phase_value = settings_ref[phase, :1, :1]
            terms = exponential_terms(wave_rows, wave_columns, phase_value)
            result = wave_exponential(planes, wave_rows, wave_columns, *terms)
            for plane in range(6):
                start = 96 * phase + LINES * plane
                rotated[start : start + LINES, lanes] = result[plane].astype(BF16)
                start = start + 192
                rotated[start : start + LINES, lanes] = alternate(result[plane], 1).astype(BF16)
    for chunk in range(2):
        columns = slice(256 * chunk, 256 * (chunk + 1))
        data = rotated[...]
        cosine = jnp.dot(data, table_ref[0, :, columns], preferred_element_type=F32)
        sine = jnp.dot(data, table_ref[1, :, columns], preferred_element_type=F32)
        for part in range(4):
            lanes = slice(LANES * (part % 2), LANES * (part % 2 + 1))
            group = 4 * (part // 2) + 2 * chunk + part % 2
            real, imag = [], []
            for field in range(6):
                start = 192 * (part // 2) + 32 * field
                top = slice(start, start + LINES)
                bottom = slice(start + LINES, start + 2 * LINES)
                real.append(cosine[top, lanes] - sine[bottom, lanes])
                imag.append(sine[top, lanes] + cosine[bottom, lanes])
            main = swap_blocks(real + imag[:2], 16)
            rest = swap_blocks([v[:8] for v in imag[2:]] + [v[8:] for v in imag[2:]], 16)
            for offset in range(8):
                message = jnp.concatenate([main[offset], rest[offset]], axis=0)
                out_ref[8 * group + offset] = message.astype(BF16)


def second_kernel(arrived_ref, table_ref, out_ref, real_part, imag_part, pairs):
    first = lanes_of(LINES) < 32
    for source in range(64):
        message = arrived_ref[source].astype(F32)
        main, rest = message[:16], message[16:]
        rest = jnp.concatenate([roll(rest, 32), roll(rest, -32)], axis=0)
        imag = jnp.where(first, roll(main, 32), rest)
        rows = slice(LINES * source, LINES * (source + 1))
        real_part[rows, :LANES] = main.astype(BF16)
        real_part[rows, LANES:] = alternate(main, 0).astype(BF16)
        imag_part[rows, :LANES] = (-imag).astype(BF16)
        imag_part[rows, LANES:] = alternate(-imag, 0).astype(BF16)
    block = lanes_of(256) // 16
    height_lanes = (block == 2) | (block == 5)
    for chunk in range(2):
        rows = slice(256 * chunk, 256 * (chunk + 1))
        grid = jnp.dot(table_ref[0, rows, :], real_part[...], preferred_element_type=F32)
        grid = grid + jnp.dot(table_ref[1, rows, :], imag_part[...], preferred_element_type=F32)
        grid = grid * (1.0 / N)
        for upper in range(2):
            part = grid[:, LANES * upper : LANES * (upper + 1)]
            target = slice(512 * upper + 256 * chunk, 512 * upper + 256 * (chunk + 1))
            other = jnp.where(height_lanes, roll(part, 32), part)
            for place, product in enumerate((part * other, part * roll(part, 16))):
                lanes = slice(LANES * place, LANES * (place + 1))
                pairs[target, lanes] = product.astype(BF16)
                lanes = slice(LANES * (place + 2), LANES * (place + 3))
                pairs[target, lanes] = alternate(product, 0).astype(BF16)
    lane = lanes_of(LINES)
    short = lanes_of(8)
    for chunk in range(2):
        rows = slice(256 * chunk, 256 * (chunk + 1))
        real = jnp.dot(table_ref[0, rows, :], pairs[...], preferred_element_type=F32)
        imag = -jnp.dot(table_ref[1, rows, :], pairs[...], preferred_element_type=F32)
        for index in range(32):
            upper, offset = index // 16, index % 16
            own = slice(LINES * offset, LINES * (offset + 1))
            main = slice(256 * upper, 256 * upper + LANES)
            rest = slice(256 * upper + LANES, 256 * (upper + 1))
            real_rest, imag_rest = real[own, rest], imag[own, rest]
            first_rows = jnp.where(lane < 96, real[own, main], roll(real_rest, 80))
            second_rows = jnp.where(lane < 96, imag[own, main], roll(imag_rest, 80))
            last_rows = jnp.where(
                short < 64,
                jnp.where(short < 32, roll(real_rest[:8], 64), roll(imag_rest[:8], -32)),
                jnp.where(short < 96, real_rest[8:], roll(imag_rest[8:], 32)),
            )
            message = jnp.concatenate([first_rows, second_rows, last_rows], axis=0)
            out_ref[32 * upper + 16 * chunk + offset] = message.astype(BF16)


PRODUCT_ORDER = ((0, 0), (0, 2), (0, 3), (1, 0), (1, 2), (1, 3), (0, 1), (0, 4))


def third_kernel(settings_ref, returned_ref, table_ref, out_ref, lines):
    wave_columns = own_columns(LINES)
    for group in range(8):
        lanes = slice(LANES * group, LANES * (group + 1))
        messages = [returned_ref[8 * group + offset].astype(F32) for offset in range(8)]
        rest = swap_blocks([message[32:] for message in messages], 16)
        for part in range(2):
            blocks = swap_blocks([m[16 * part : 16 * (part + 1)] for m in messages], 16)
            places = list(PRODUCT_ORDER) + [(1, 1), (1, 4)]
            blocks.append(jnp.concatenate([rest[2 * part], rest[4 + 2 * part]], axis=0))
            blocks.append(jnp.concatenate([rest[2 * part + 1], rest[5 + 2 * part]], axis=0))
            for (phase, product), block in zip(places, blocks):
                start = 160 * part + 80 * phase + LINES * product
                lines[start : start + LINES, lanes] = block.astype(BF16)
                start = start + 320
                lines[start : start + LINES, lanes] = alternate(block, 1).astype(BF16)
    for chunk in range(2):
        columns = slice(256 * chunk, 256 * (chunk + 1))
        data = lines[...]
        cosine = jnp.dot(data, table_ref[0, :, columns], preferred_element_type=F32)
        sine = jnp.dot(data, table_ref[1, :, columns], preferred_element_type=F32)
        for part in range(4):
            lanes = slice(LANES * (part % 2), LANES * (part % 2 + 1))
            group = 4 * (part // 2) + 2 * chunk + part % 2
            wave_rows = wave_of(lanes_of(LINES) + LANES * group)
            total = None
            for phase in range(2):
                phase_value = settings_ref[phase, :1, :1]
                weight = settings_ref[phase, :1, 64:65]
                real, imag = [], []
                for product in range(5):
                    start = 320 * (part // 2) + 80 * phase + LINES * product
                    top = slice(start, start + LINES)
                    bottom = slice(160 + start, 160 + start + LINES)
                    real.append((cosine[top, lanes] + sine[bottom, lanes]) * (1.0 / N))
                    imag.append((cosine[bottom, lanes] - sine[top, lanes]) * (1.0 / N))
                tendency = []
                for toward_east, toward_north in ((0, 1), (1, 2), (3, 4)):
                    tendency.append(wave_rows * imag[toward_east] + wave_columns * imag[toward_north])
                    tendency.append(
                        -(wave_rows * real[toward_east] + wave_columns * real[toward_north])
                    )
                sine_term, cosine_term = exponential_terms(wave_rows, wave_columns, phase_value)
                result = wave_exponential(
                    tendency, wave_rows, wave_columns, -sine_term, cosine_term
                )
                result = [weight * plane for plane in result]
                total = result if total is None else [a + b for a, b in zip(total, result)]
            main = swap_blocks(total[:4], 32)
            rest = swap_blocks([total[4][:8], total[5][:8], total[4][8:], total[5][8:]], 32)
            for offset in range(4):
                message = jnp.concatenate([main[offset], rest[offset]], axis=0)
                out_ref[slot(4 * group + offset)] = message.astype(BF16)


def last_kernel(state_ref, parts_ref, out_ref):
    mains, rests = [], []
    for part in range(4):
        total = parts_ref[slot(part)].astype(F32)
        for block in range(1, 8):
            total = total + parts_ref[slot(4 * block + part)].astype(F32)
        mains.append(total[:16])
        rests.append(jnp.concatenate([total[16:], roll(total[16:], 64)], axis=0))
    turned = jnp.concatenate(mains + rests, axis=0).T
    row_start = (own_block() * 4 + lax.axis_index("zm") * 2 + lax.axis_index("yh")) * ROWS
    column_start = (lax.axis_index("xy") * 2 + lax.axis_index("c")) * 64
    wave_rows = wave_of(lax.broadcasted_iota(jnp.int32, (ROWS, 64), 0) + row_start)
    wave_columns = wave_of(lax.broadcasted_iota(jnp.int32, (ROWS, 64), 1) + column_start)
    fields = []
    for plane in range(6):
        rows = slice(ROWS * (plane % 4), ROWS * (plane % 4 + 1))
        total = turned[rows, :64] if plane < 4 else turned[rows, 64:]
        fields.append(state_ref[plane // 2, plane % 2] + time_step * total)
    terms = exponential_terms(wave_rows, wave_columns, time_step)
    result = wave_exponential(fields, wave_rows, wave_columns, *terms)
    for plane in range(6):
        out_ref[plane // 2, plane % 2] = result[plane]


def call(kernel, name, shape, dtype, scratch, places, flops, outs=None):
    spots = [pl.BlockSpec(memory_space=pltpu.SMEM if p == "s" else pltpu.VMEM) for p in places]
    whole = pl.BlockSpec(memory_space=pltpu.VMEM)
    shapes = jax.ShapeDtypeStruct(shape, dtype)
    extra = jax.ShapeDtypeStruct((8, LANES), F32)
    return pl.pallas_call(
        kernel,
        name=name,
        out_shape=(shapes, extra) if outs else shapes,
        in_specs=spots,
        out_specs=(whole, whole) if outs else whole,
        scratch_shapes=[pltpu.VMEM(s, BF16) for s in scratch],
        cost_estimate=pl.CostEstimate(flops=flops, bytes_accessed=1 << 20, transcendentals=0),
        compiler_params=pltpu.CompilerParams(vmem_limit_bytes=VMEM_LIMIT),
    )


def per_device(spectral_state, phase_index, weight_count):
    tables, turned_tables = fourier_tables()
    spread, settings = call(
        spread_kernel, "spread", (32, 24, LANES), BF16, [], "ssv", 1 << 33, True
    )(phase_index, weight_count, spectral_state)
    settings = lax.all_gather(settings, "c")
    settings = lax.ppermute(
        settings, ("xy", "zh", "zl"), [(8 * i + j, 8 * j + i) for i in range(8) for j in range(8)]
    )
    gathered = lax.all_to_all(spread, MAIN_AXES, 0, 0)
    outgoing = call(first_kernel, "inverse_rows", (64, 24, LANES), BF16, [(384, N)], "vvv", 1 << 30)(
        settings, gathered, tables
    )
    arrived = lax.all_to_all(outgoing, GROUP_AXES, 0, 0)
    outgoing_back = call(
        second_kernel,
        "grid_products",
        (64, 40, LANES),
        BF16,
        [(N, 2 * LANES), (N, 2 * LANES), (N, 4 * LANES)],
        "vv",
        1 << 30,
    )(arrived, turned_tables)
    returned = lax.all_to_all(outgoing_back, GROUP_AXES, 0, 0)
    weighted = call(third_kernel, "forward_rows", (32, 24, LANES), BF16, [(640, N)], "vvv", 1 << 31)(
        settings, returned, tables
    )
    parts = lax.all_to_all(weighted, MAIN_AXES, 0, 0)
    return call(last_kernel, "advance", spectral_state.shape, F32, [], "vv", 1 << 24)(spectral_state, parts)


def solution(mesh):
    fine = Mesh(mesh.devices.reshape(8, 2, 2, 4, 2, 2), ("xy", "c", "zh", "zl", "zm", "yh"))
    rows, columns = ("zh", "zl", "zm", "yh"), ("xy", "c")
    in_specs = (P(None, None, rows, columns), P(columns), P(columns))
    out_specs = P(None, None, rows, columns)
    return jax.shard_map(
        per_device, mesh=fine, in_specs=in_specs, out_specs=out_specs, check_vma=False
    )
```

```python
import math

import jax
import jax.numpy as jnp
import numpy as np
from jax import lax
from jax.experimental import pallas as pl
from jax.experimental.pallas import tpu as pltpu
from jax.sharding import Mesh
from jax.sharding import PartitionSpec as P

N = 1024
LANES = 128
ROWS = 32
LINES = 16

coriolis = 1.0
wave_speed = 6.0
phase_step = 0.25
time_step = 2.0
weight_scale = 64.0

VMEM_LIMIT = 28 * 1024 * 1024
F32 = jnp.float32
BF16 = jnp.bfloat16
MAIN_AXES = ("zl", "zm", "zh", "yh")
GROUP_AXES = ("xy", "c", "zm", "yh")


def fourier_tables():
    product = np.arange(N)[:, None] * np.arange(N // 2)[None, :] % N
    angles = product.astype(np.float64) * (2.0 * math.pi / N)
    tables = np.stack([np.cos(angles), np.sin(angles)])
    return jnp.asarray(tables, BF16), jnp.asarray(tables.transpose(0, 2, 1), BF16)


def wave_of(index):
    shifted = jnp.where(index >= N // 2, index - N, index)
    return shifted.astype(F32) * (2.0 / N)


def sine_cosine(angle):
    turns = jnp.floor(angle * (2.0 / math.pi) + 0.5)
    rest = angle - turns * 1.5703125
    rest = rest - turns * 4.837512969970703125e-4
    rest = rest - turns * 7.54978995489188216e-8
    square = rest * rest
    sine = ((-1.9515295891e-4 * square + 8.3321608736e-3) * square - 1.6666654611e-1) * square * rest + rest
    cosine = ((2.443315711809948e-5 * square - 1.388731625493765e-3) * square + 4.166664568298827e-2) * square * square
    cosine = cosine - 0.5 * square + 1.0
    quarter = turns.astype(jnp.int32)
    odd = (quarter & 1) == 1
    sine_out = jnp.where(odd, cosine, sine)
    cosine_out = jnp.where(odd, sine, cosine)
    sine_out = jnp.where((quarter & 2) == 2, -sine_out, sine_out)
    cosine_out = jnp.where(((quarter + 1) & 2) == 2, -cosine_out, cosine_out)
    return sine_out, cosine_out


def exponential_terms(wave_rows, wave_columns, phase_value):
    squared = coriolis * coriolis + (wave_speed * wave_speed) * (
        wave_rows * wave_rows + wave_columns * wave_columns
    )
    inverse = lax.rsqrt(squared)
    inverse = inverse * (1.5 - 0.5 * squared * inverse * inverse)
    sine, cosine = sine_cosine(squared * inverse * phase_value)
    return sine * inverse, (1.0 - cosine) * (inverse * inverse)


def wave_operator(fields, speed_rows, speed_columns):
    east_r, east_i, north_r, north_i, height_r, height_i = fields
    return (
        coriolis * north_r + speed_rows * height_i,
        coriolis * north_i - speed_rows * height_r,
        speed_columns * height_i - coriolis * east_r,
        -speed_columns * height_r - coriolis * east_i,
        speed_rows * east_i + speed_columns * north_i,
        -(speed_rows * east_r + speed_columns * north_r),
    )


def wave_exponential(fields, wave_rows, wave_columns, sine_term, cosine_term):
    speed_rows = wave_speed * wave_rows
    speed_columns = wave_speed * wave_columns
    single = wave_operator(fields, speed_rows, speed_columns)
    double = wave_operator(single, speed_rows, speed_columns)
    return [w + sine_term * a + cosine_term * b for w, a, b in zip(fields, single, double)]


def lanes_of(rows):
    return lax.broadcasted_iota(jnp.int32, (rows, LANES), 1)


def roll(values, shift):
    return pltpu.roll(values, shift % LANES, 1)


def swap_blocks(parts, width):
    parts = list(parts)
    lane = lanes_of(parts[0].shape[0])
    step = 1
    while step < len(parts):
        shift = width * step
        odd = (lane & shift) == shift
        for low in range(len(parts)):
            if low & step:
                continue
            high = low | step
            parts[low], parts[high] = (
                jnp.where(odd, roll(parts[high], shift), parts[low]),
                jnp.where(odd, parts[high], roll(parts[low], -shift)),
            )
        step *= 2
    return parts


def slot(device):
    high, low, rest = device // 16, device // 4 % 4, device % 4
    return low * 8 + rest // 2 * 4 + high * 2 + rest % 2


def own_block():
    return 4 * lax.axis_index("zh") + lax.axis_index("zl")


def alternate(values, axis):
    index = lax.broadcasted_iota(jnp.int32, values.shape, axis)
    return jnp.where((index & 1) == 1, -values, values)


def own_columns(rows):
    device = (lax.axis_index("xy") * 2 + lax.axis_index("c")) * 4
    device = device + lax.axis_index("zm") * 2 + lax.axis_index("yh")
    return wave_of(lax.broadcasted_iota(jnp.int32, (rows, LANES), 0) + device * LINES)


def settings_kernel(phase_ref, weight_ref, settings_ref):
    phase_value = phase_ref[0].astype(F32) * phase_step
    weight = weight_ref[0].astype(F32) * (1.0 / weight_scale)
    settings_ref[...] = jnp.where(lanes_of(8) < 64, phase_value, weight)


def spread_kernel(state_ref, out_ref):
    def plane(index):
        return state_ref[index // 2, index % 2]

    left = jnp.concatenate([plane(index) for index in range(4)], axis=0)
    right = jnp.concatenate([plane(4), plane(5), jnp.zeros((64, 64), F32)], axis=0)
    turned = jnp.concatenate([left, right], axis=1).T
    low = lanes_of(8) < 64
    for part in range(4):
        main = turned[LINES * part : LINES * (part + 1)]
        rest = turned[64 + LINES * part : 64 + LINES * (part + 1)]
        rest = jnp.where(low, rest[:8], roll(rest[8:], 64))
        message = jnp.concatenate([main, rest], axis=0).astype(BF16)
        for block in range(8):
            out_ref[slot(4 * block + part)] = message


def first_kernel(settings_ref, gathered_ref, table_ref, out_ref, rotated):
    wave_columns = own_columns(LINES)
    for group in range(8):
        lanes = slice(LANES * group, LANES * (group + 1))
        messages = [gathered_ref[slot(4 * group + offset)].astype(F32) for offset in range(4)]
        planes = swap_blocks([message[:16] for message in messages], 32)
        rest = swap_blocks([message[16:] for message in messages], 32)
        planes.append(jnp.concatenate([rest[0], rest[2]], axis=0))
        planes.append(jnp.concatenate([rest[1], rest[3]], axis=0))
        wave_rows = wave_of(lanes_of(LINES) + LANES * group)
        for phase in range(2):
            phase_value = settings_ref[phase, :1, :1]
            terms = exponential_terms(wave_rows, wave_columns, phase_value)
            result = wave_exponential(planes, wave_rows, wave_columns, *terms)
            for plane in range(6):
                start = 96 * phase + LINES * plane
                rotated[start : start + LINES, lanes] = result[plane].astype(BF16)
                start = start + 192
                rotated[start : start + LINES, lanes] = alternate(result[plane], 1).astype(BF16)
    for chunk in range(2):
        columns = slice(256 * chunk, 256 * (chunk + 1))
        data = rotated[...]
        cosine = jnp.dot(data, table_ref[0, :, columns], preferred_element_type=F32)
        sine = jnp.dot(data, table_ref[1, :, columns], preferred_element_type=F32)
        for part in range(4):
            lanes = slice(LANES * (part % 2), LANES * (part % 2 + 1))
            group = 4 * (part // 2) + 2 * chunk + part % 2
            real, imag = [], []
            for field in range(6):
                start = 192 * (part // 2) + 32 * field
                top = slice(start, start + LINES)
                bottom = slice(start + LINES, start + 2 * LINES)
                real.append(cosine[top, lanes] - sine[bottom, lanes])
                imag.append(sine[top, lanes] + cosine[bottom, lanes])
            main = swap_blocks(real + imag[:2], 16)
            rest = swap_blocks([v[:8] for v in imag[2:]] + [v[8:] for v in imag[2:]], 16)
            for offset in range(8):
                message = jnp.concatenate([main[offset], rest[offset]], axis=0)
                out_ref[8 * group + offset] = message.astype(BF16)


def second_kernel(arrived_ref, table_ref, out_ref, real_part, imag_part, pairs):
    first = lanes_of(LINES) < 32
    for source in range(64):
        message = arrived_ref[source].astype(F32)
        main, rest = message[:16], message[16:]
        rest = jnp.concatenate([roll(rest, 32), roll(rest, -32)], axis=0)
        imag = jnp.where(first, roll(main, 32), rest)
        rows = slice(LINES * source, LINES * (source + 1))
        real_part[rows, :LANES] = main.astype(BF16)
        real_part[rows, LANES:] = alternate(main, 0).astype(BF16)
        imag_part[rows, :LANES] = (-imag).astype(BF16)
        imag_part[rows, LANES:] = alternate(-imag, 0).astype(BF16)
    block = lanes_of(256) // 16
    height_lanes = (block == 2) | (block == 5)
    for chunk in range(2):
        rows = slice(256 * chunk, 256 * (chunk + 1))
        grid = jnp.dot(table_ref[0, rows, :], real_part[...], preferred_element_type=F32)
        grid = grid + jnp.dot(table_ref[1, rows, :], imag_part[...], preferred_element_type=F32)
        grid = grid * (1.0 / N)
        for upper in range(2):
            part = grid[:, LANES * upper : LANES * (upper + 1)]
            target = slice(512 * upper + 256 * chunk, 512 * upper + 256 * (chunk + 1))
            other = jnp.where(height_lanes, roll(part, 32), part)
            for place, product in enumerate((part * other, part * roll(part, 16))):
                lanes = slice(LANES * place, LANES * (place + 1))
                pairs[target, lanes] = product.astype(BF16)
                lanes = slice(LANES * (place + 2), LANES * (place + 3))
                pairs[target, lanes] = alternate(product, 0).astype(BF16)
    lane = lanes_of(LINES)
    short = lanes_of(8)
    for chunk in range(2):
        rows = slice(256 * chunk, 256 * (chunk + 1))
        real = jnp.dot(table_ref[0, rows, :], pairs[...], preferred_element_type=F32)
        imag = -jnp.dot(table_ref[1, rows, :], pairs[...], preferred_element_type=F32)
        for index in range(32):
            upper, offset = index // 16, index % 16
            own = slice(LINES * offset, LINES * (offset + 1))
            main = slice(256 * upper, 256 * upper + LANES)
            rest = slice(256 * upper + LANES, 256 * (upper + 1))
            real_rest, imag_rest = real[own, rest], imag[own, rest]
            first_rows = jnp.where(lane < 96, real[own, main], roll(real_rest, 80))
            second_rows = jnp.where(lane < 96, imag[own, main], roll(imag_rest, 80))
            last_rows = jnp.where(
                short < 64,
                jnp.where(short < 32, roll(real_rest[:8], 64), roll(imag_rest[:8], -32)),
                jnp.where(short < 96, real_rest[8:], roll(imag_rest[8:], 32)),
            )
            message = jnp.concatenate([first_rows, second_rows, last_rows], axis=0)
            out_ref[32 * upper + 16 * chunk + offset] = message.astype(BF16)


PRODUCT_ORDER = ((0, 0), (0, 2), (0, 3), (1, 0), (1, 2), (1, 3), (0, 1), (0, 4))


def third_kernel(settings_ref, returned_ref, table_ref, out_ref, lines):
    wave_columns = own_columns(LINES)
    for group in range(8):
        lanes = slice(LANES * group, LANES * (group + 1))
        messages = [returned_ref[8 * group + offset].astype(F32) for offset in range(8)]
        rest = swap_blocks([message[32:] for message in messages], 16)
        for part in range(2):
            blocks = swap_blocks([m[16 * part : 16 * (part + 1)] for m in messages], 16)
            places = list(PRODUCT_ORDER) + [(1, 1), (1, 4)]
            blocks.append(jnp.concatenate([rest[2 * part], rest[4 + 2 * part]], axis=0))
            blocks.append(jnp.concatenate([rest[2 * part + 1], rest[5 + 2 * part]], axis=0))
            for (phase, product), block in zip(places, blocks):
                start = 160 * part + 80 * phase + LINES * product
                lines[start : start + LINES, lanes] = block.astype(BF16)
                start = start + 320
                lines[start : start + LINES, lanes] = alternate(block, 1).astype(BF16)
    for chunk in range(2):
        columns = slice(256 * chunk, 256 * (chunk + 1))
        data = lines[...]
        cosine = jnp.dot(data, table_ref[0, :, columns], preferred_element_type=F32)
        sine = jnp.dot(data, table_ref[1, :, columns], preferred_element_type=F32)
        for part in range(4):
            lanes = slice(LANES * (part % 2), LANES * (part % 2 + 1))
            group = 4 * (part // 2) + 2 * chunk + part % 2
            wave_rows = wave_of(lanes_of(LINES) + LANES * group)
            total = None
            for phase in range(2):
                phase_value = settings_ref[phase, :1, :1]
                weight = settings_ref[phase, :1, 64:65]
                real, imag = [], []
                for product in range(5):
                    start = 320 * (part // 2) + 80 * phase + LINES * product
                    top = slice(start, start + LINES)
                    bottom = slice(160 + start, 160 + start + LINES)
                    real.append((cosine[top, lanes] + sine[bottom, lanes]) * (1.0 / N))
                    imag.append((cosine[bottom, lanes] - sine[top, lanes]) * (1.0 / N))
                tendency = []
                for toward_east, toward_north in ((0, 1), (1, 2), (3, 4)):
                    tendency.append(wave_rows * imag[toward_east] + wave_columns * imag[toward_north])
                    tendency.append(
                        -(wave_rows * real[toward_east] + wave_columns * real[toward_north])
                    )
                sine_term, cosine_term = exponential_terms(wave_rows, wave_columns, phase_value)
                result = wave_exponential(
                    tendency, wave_rows, wave_columns, -sine_term, cosine_term
                )
                result = [weight * plane for plane in result]
                total = result if total is None else [a + b for a, b in zip(total, result)]
            main = swap_blocks(total[:4], 32)
            rest = swap_blocks([total[4][:8], total[5][:8], total[4][8:], total[5][8:]], 32)
            for offset in range(4):
                message = jnp.concatenate([main[offset], rest[offset]], axis=0)
                out_ref[slot(4 * group + offset)] = message.astype(BF16)


def last_kernel(state_ref, parts_ref, out_ref):
    mains, rests = [], []
    for part in range(4):
        total = parts_ref[slot(part)].astype(F32)
        for block in range(1, 8):
            total = total + parts_ref[slot(4 * block + part)].astype(F32)
        mains.append(total[:16])
        rests.append(jnp.concatenate([total[16:], roll(total[16:], 64)], axis=0))
    turned = jnp.concatenate(mains + rests, axis=0).T
    row_start = (own_block() * 4 + lax.axis_index("zm") * 2 + lax.axis_index("yh")) * ROWS
    column_start = (lax.axis_index("xy") * 2 + lax.axis_index("c")) * 64
    wave_rows = wave_of(lax.broadcasted_iota(jnp.int32, (ROWS, 64), 0) + row_start)
    wave_columns = wave_of(lax.broadcasted_iota(jnp.int32, (ROWS, 64), 1) + column_start)
    fields = []
    for plane in range(6):
        rows = slice(ROWS * (plane % 4), ROWS * (plane % 4 + 1))
        total = turned[rows, :64] if plane < 4 else turned[rows, 64:]
        fields.append(state_ref[plane // 2, plane % 2] + time_step * total)
    terms = exponential_terms(wave_rows, wave_columns, time_step)
    result = wave_exponential(fields, wave_rows, wave_columns, *terms)
    for plane in range(6):
        out_ref[plane // 2, plane % 2] = result[plane]


def call(kernel, name, shape, dtype, scratch, places, flops):
    spots = [pl.BlockSpec(memory_space=pltpu.SMEM if p == "s" else pltpu.VMEM) for p in places]
    return pl.pallas_call(
        kernel,
        name=name,
        out_shape=jax.ShapeDtypeStruct(shape, dtype),
        in_specs=spots,
        out_specs=pl.BlockSpec(memory_space=pltpu.VMEM),
        scratch_shapes=[pltpu.VMEM(s, BF16) for s in scratch],
        cost_estimate=pl.CostEstimate(flops=flops, bytes_accessed=1 << 20, transcendentals=0),
        compiler_params=pltpu.CompilerParams(vmem_limit_bytes=VMEM_LIMIT),
    )


def per_device(spectral_state, phase_index, weight_count):
    tables, turned_tables = fourier_tables()
    spread = call(spread_kernel, "spread", (32, 24, LANES), BF16, [], "v", 1 << 33)(spectral_state)
    settings = call(settings_kernel, "settings", (8, LANES), F32, [], "ss", 1 << 12)(
        phase_index, weight_count
    )
    settings = lax.all_gather(settings, "c")
    settings = lax.ppermute(
        settings, ("xy", "zh", "zl"), [(8 * i + j, 8 * j + i) for i in range(8) for j in range(8)]
    )
    gathered = lax.all_to_all(spread, MAIN_AXES, 0, 0)
    outgoing = call(first_kernel, "inverse_rows", (64, 24, LANES), BF16, [(384, N)], "vvv", 1 << 30)(
        settings, gathered, tables
    )
    arrived = lax.all_to_all(outgoing, GROUP_AXES, 0, 0)
    outgoing_back = call(
        second_kernel,
        "grid_products",
        (64, 40, LANES),
        BF16,
        [(N, 2 * LANES), (N, 2 * LANES), (N, 4 * LANES)],
        "vv",
        1 << 30,
    )(arrived, turned_tables)
    returned = lax.all_to_all(outgoing_back, GROUP_AXES, 0, 0)
    weighted = call(third_kernel, "forward_rows", (32, 24, LANES), BF16, [(640, N)], "vvv", 1 << 31)(
        settings, returned, tables
    )
    parts = lax.all_to_all(weighted, MAIN_AXES, 0, 0)
    return call(last_kernel, "advance", spectral_state.shape, F32, [], "vv", 1 << 24)(spectral_state, parts)


def solution(mesh):
    fine = Mesh(mesh.devices.reshape(8, 2, 2, 4, 2, 2), ("xy", "c", "zh", "zl", "zm", "yh"))
    rows, columns = ("zh", "zl", "zm", "yh"), ("xy", "c")
    in_specs = (P(None, None, rows, columns), P(columns), P(columns))
    out_specs = P(None, None, rows, columns)
    return jax.shard_map(
        per_device, mesh=fine, in_specs=in_specs, out_specs=out_specs, check_vma=False
    )
```

```python
import math

import jax
import jax.numpy as jnp
import numpy as np
from jax import lax
from jax.experimental import pallas as pl
from jax.experimental.pallas import tpu as pltpu
from jax.sharding import Mesh
from jax.sharding import PartitionSpec as P

N = 1024
LANES = 128
ROWS = 32
LINES = 16

coriolis = 1.0
wave_speed = 6.0
phase_step = 0.25
time_step = 2.0
weight_scale = 64.0

VMEM_LIMIT = 28 * 1024 * 1024
F32 = jnp.float32
BF16 = jnp.bfloat16
MAIN_AXES = ("zl", "zm", "zh", "yh")
GROUP_AXES = ("xy", "c", "zm", "yh")


def fourier_tables():
    product = np.arange(N)[:, None] * np.arange(N // 2)[None, :] % N
    angles = product.astype(np.float64) * (2.0 * math.pi / N)
    tables = np.stack([np.cos(angles), np.sin(angles)])
    return jnp.asarray(tables, BF16), jnp.asarray(tables.transpose(0, 2, 1), BF16)


def wave_of(index):
    shifted = jnp.where(index >= N // 2, index - N, index)
    return shifted.astype(F32) * (2.0 / N)


def sine_cosine(angle):
    turns = jnp.floor(angle * (2.0 / math.pi) + 0.5)
    rest = angle - turns * 1.5703125
    rest = rest - turns * 4.837512969970703125e-4
    rest = rest - turns * 7.54978995489188216e-8
    square = rest * rest
    sine = ((-1.9515295891e-4 * square + 8.3321608736e-3) * square - 1.6666654611e-1) * square * rest + rest
    cosine = ((2.443315711809948e-5 * square - 1.388731625493765e-3) * square + 4.166664568298827e-2) * square * square
    cosine = cosine - 0.5 * square + 1.0
    quarter = turns.astype(jnp.int32)
    odd = (quarter & 1) == 1
    sine_out = jnp.where(odd, cosine, sine)
    cosine_out = jnp.where(odd, sine, cosine)
    sine_out = jnp.where((quarter & 2) == 2, -sine_out, sine_out)
    cosine_out = jnp.where(((quarter + 1) & 2) == 2, -cosine_out, cosine_out)
    return sine_out, cosine_out


def exponential_terms(wave_rows, wave_columns, phase_value):
    squared = coriolis * coriolis + (wave_speed * wave_speed) * (
        wave_rows * wave_rows + wave_columns * wave_columns
    )
    inverse = lax.rsqrt(squared)
    inverse = inverse * (1.5 - 0.5 * squared * inverse * inverse)
    sine, cosine = sine_cosine(squared * inverse * phase_value)
    return sine * inverse, (1.0 - cosine) * (inverse * inverse)


def wave_operator(fields, speed_rows, speed_columns):
    east_r, east_i, north_r, north_i, height_r, height_i = fields
    return (
        coriolis * north_r + speed_rows * height_i,
        coriolis * north_i - speed_rows * height_r,
        speed_columns * height_i - coriolis * east_r,
        -speed_columns * height_r - coriolis * east_i,
        speed_rows * east_i + speed_columns * north_i,
        -(speed_rows * east_r + speed_columns * north_r),
    )


def wave_exponential(fields, wave_rows, wave_columns, sine_term, cosine_term):
    speed_rows = wave_speed * wave_rows
    speed_columns = wave_speed * wave_columns
    single = wave_operator(fields, speed_rows, speed_columns)
    double = wave_operator(single, speed_rows, speed_columns)
    return [w + sine_term * a + cosine_term * b for w, a, b in zip(fields, single, double)]


def lanes_of(rows):
    return lax.broadcasted_iota(jnp.int32, (rows, LANES), 1)


def roll(values, shift):
    return pltpu.roll(values, shift % LANES, 1)


def swap_blocks(parts, width):
    parts = list(parts)
    lane = lanes_of(parts[0].shape[0])
    step = 1
    while step < len(parts):
        shift = width * step
        odd = (lane & shift) == shift
        for low in range(len(parts)):
            if low & step:
                continue
            high = low | step
            parts[low], parts[high] = (
                jnp.where(odd, roll(parts[high], shift), parts[low]),
                jnp.where(odd, parts[high], roll(parts[low], -shift)),
            )
        step *= 2
    return parts


def slot(device):
    high, low, rest = device // 16, device // 4 % 4, device % 4
    return low * 8 + rest // 2 * 4 + high * 2 + rest % 2


def own_block():
    return 4 * lax.axis_index("zh") + lax.axis_index("zl")


def alternate(values, axis):
    index = lax.broadcasted_iota(jnp.int32, values.shape, axis)
    return jnp.where((index & 1) == 1, -values, values)


def own_columns(rows):
    device = (lax.axis_index("xy") * 2 + lax.axis_index("c")) * 4
    device = device + lax.axis_index("zm") * 2 + lax.axis_index("yh")
    return wave_of(lax.broadcasted_iota(jnp.int32, (rows, LANES), 0) + device * LINES)


def settings_kernel(phase_ref, weight_ref, settings_ref):
    phase_value = phase_ref[0].astype(F32) * phase_step
    weight = weight_ref[0].astype(F32) * (1.0 / weight_scale)
    settings_ref[...] = jnp.where(lanes_of(8) < 64, phase_value, weight)


def spread_kernel(state_ref, out_ref):
    def plane(index):
        return state_ref[index // 2, index % 2]

    left = jnp.concatenate([plane(index) for index in range(4)], axis=0)
    right = jnp.concatenate([plane(4), plane(5), jnp.zeros((64, 64), F32)], axis=0)
    turned = jnp.concatenate([left, right], axis=1).T
    low = lanes_of(8) < 64
    for part in range(4):
        main = turned[LINES * part : LINES * (part + 1)]
        rest = turned[64 + LINES * part : 64 + LINES * (part + 1)]
        rest = jnp.where(low, rest[:8], roll(rest[8:], 64))
        message = jnp.concatenate([main, rest], axis=0).astype(BF16)
        for block in range(8):
            out_ref[slot(4 * block + part)] = message


def first_kernel(settings_ref, gathered_ref, table_ref, out_ref, terms_ref, rotated):
    wave_columns = own_columns(LINES)
    for group in range(8):
        lanes = slice(LANES * group, LANES * (group + 1))
        messages = [gathered_ref[slot(4 * group + offset)].astype(F32) for offset in range(4)]
        planes = swap_blocks([message[:16] for message in messages], 32)
        rest = swap_blocks([message[16:] for message in messages], 32)
        planes.append(jnp.concatenate([rest[0], rest[2]], axis=0))
        planes.append(jnp.concatenate([rest[1], rest[3]], axis=0))
        wave_rows = wave_of(lanes_of(LINES) + LANES * group)
        for phase in range(2):
            phase_value = settings_ref[phase, :1, :1]
            terms = exponential_terms(wave_rows, wave_columns, phase_value)
            terms_ref[2 * phase, :, lanes], terms_ref[2 * phase + 1, :, lanes] = terms
            result = wave_exponential(planes, wave_rows, wave_columns, *terms)
            for plane in range(6):
                start = 96 * phase + LINES * plane
                rotated[start : start + LINES, lanes] = result[plane].astype(BF16)
                start = start + 192
                rotated[start : start + LINES, lanes] = alternate(result[plane], 1).astype(BF16)
    for chunk in range(2):
        columns = slice(256 * chunk, 256 * (chunk + 1))
        data = rotated[...]
        cosine = jnp.dot(data, table_ref[0, :, columns], preferred_element_type=F32)
        sine = jnp.dot(data, table_ref[1, :, columns], preferred_element_type=F32)
        for part in range(4):
            lanes = slice(LANES * (part % 2), LANES * (part % 2 + 1))
            group = 4 * (part // 2) + 2 * chunk + part % 2
            real, imag = [], []
            for field in range(6):
                start = 192 * (part // 2) + 32 * field
                top = slice(start, start + LINES)
                bottom = slice(start + LINES, start + 2 * LINES)
                real.append(cosine[top, lanes] - sine[bottom, lanes])
                imag.append(sine[top, lanes] + cosine[bottom, lanes])
            main = swap_blocks(real + imag[:2], 16)
            rest = swap_blocks([v[:8] for v in imag[2:]] + [v[8:] for v in imag[2:]], 16)
            for offset in range(8):
                message = jnp.concatenate([main[offset], rest[offset]], axis=0)
                out_ref[8 * group + offset] = message.astype(BF16)


def second_kernel(arrived_ref, table_ref, out_ref, real_part, imag_part, pairs):
    first = lanes_of(LINES) < 32
    for source in range(64):
        message = arrived_ref[source].astype(F32)
        main, rest = message[:16], message[16:]
        rest = jnp.concatenate([roll(rest, 32), roll(rest, -32)], axis=0)
        imag = jnp.where(first, roll(main, 32), rest)
        rows = slice(LINES * source, LINES * (source + 1))
        real_part[rows, :LANES] = main.astype(BF16)
        real_part[rows, LANES:] = alternate(main, 0).astype(BF16)
        imag_part[rows, :LANES] = (-imag).astype(BF16)
        imag_part[rows, LANES:] = alternate(-imag, 0).astype(BF16)
    block = lanes_of(256) // 16
    height_lanes = (block == 2) | (block == 5)
    for chunk in range(2):
        rows = slice(256 * chunk, 256 * (chunk + 1))
        grid = jnp.dot(table_ref[0, rows, :], real_part[...], preferred_element_type=F32)
        grid = grid + jnp.dot(table_ref[1, rows, :], imag_part[...], preferred_element_type=F32)
        grid = grid * (1.0 / N)
        for upper in range(2):
            part = grid[:, LANES * upper : LANES * (upper + 1)]
            target = slice(512 * upper + 256 * chunk, 512 * upper + 256 * (chunk + 1))
            other = jnp.where(height_lanes, roll(part, 32), part)
            for place, product in enumerate((part * other, part * roll(part, 16))):
                lanes = slice(LANES * place, LANES * (place + 1))
                pairs[target, lanes] = product.astype(BF16)
                lanes = slice(LANES * (place + 2), LANES * (place + 3))
                pairs[target, lanes] = alternate(product, 0).astype(BF16)
    lane = lanes_of(LINES)
    short = lanes_of(8)
    for chunk in range(2):
        rows = slice(256 * chunk, 256 * (chunk + 1))
        real = jnp.dot(table_ref[0, rows, :], pairs[...], preferred_element_type=F32)
        imag = -jnp.dot(table_ref[1, rows, :], pairs[...], preferred_element_type=F32)
        for index in range(32):
            upper, offset = index // 16, index % 16
            own = slice(LINES * offset, LINES * (offset + 1))
            main = slice(256 * upper, 256 * upper + LANES)
            rest = slice(256 * upper + LANES, 256 * (upper + 1))
            real_rest, imag_rest = real[own, rest], imag[own, rest]
            first_rows = jnp.where(lane < 96, real[own, main], roll(real_rest, 80))
            second_rows = jnp.where(lane < 96, imag[own, main], roll(imag_rest, 80))
            last_rows = jnp.where(
                short < 64,
                jnp.where(short < 32, roll(real_rest[:8], 64), roll(imag_rest[:8], -32)),
                jnp.where(short < 96, real_rest[8:], roll(imag_rest[8:], 32)),
            )
            message = jnp.concatenate([first_rows, second_rows, last_rows], axis=0)
            out_ref[32 * upper + 16 * chunk + offset] = message.astype(BF16)


PRODUCT_ORDER = ((0, 0), (0, 2), (0, 3), (1, 0), (1, 2), (1, 3), (0, 1), (0, 4))


def third_kernel(settings_ref, terms_ref, returned_ref, table_ref, out_ref, lines):
    wave_columns = own_columns(LINES)
    for group in range(8):
        lanes = slice(LANES * group, LANES * (group + 1))
        messages = [returned_ref[8 * group + offset].astype(F32) for offset in range(8)]
        rest = swap_blocks([message[32:] for message in messages], 16)
        for part in range(2):
            blocks = swap_blocks([m[16 * part : 16 * (part + 1)] for m in messages], 16)
            places = list(PRODUCT_ORDER) + [(1, 1), (1, 4)]
            blocks.append(jnp.concatenate([rest[2 * part], rest[4 + 2 * part]], axis=0))
            blocks.append(jnp.concatenate([rest[2 * part + 1], rest[5 + 2 * part]], axis=0))
            for (phase, product), block in zip(places, blocks):
                start = 160 * part + 80 * phase + LINES * product
                lines[start : start + LINES, lanes] = block.astype(BF16)
                start = start + 320
                lines[start : start + LINES, lanes] = alternate(block, 1).astype(BF16)
    for chunk in range(2):
        columns = slice(256 * chunk, 256 * (chunk + 1))
        data = lines[...]
        cosine = jnp.dot(data, table_ref[0, :, columns], preferred_element_type=F32)
        sine = jnp.dot(data, table_ref[1, :, columns], preferred_element_type=F32)
        for part in range(4):
            lanes = slice(LANES * (part % 2), LANES * (part % 2 + 1))
            group = 4 * (part // 2) + 2 * chunk + part % 2
            wave_rows = wave_of(lanes_of(LINES) + LANES * group)
            total = None
            for phase in range(2):
                weight = settings_ref[phase, :1, 64:65]
                real, imag = [], []
                for product in range(5):
                    start = 320 * (part // 2) + 80 * phase + LINES * product
                    top = slice(start, start + LINES)
                    bottom = slice(160 + start, 160 + start + LINES)
                    real.append((cosine[top, lanes] + sine[bottom, lanes]) * (1.0 / N))
                    imag.append((cosine[bottom, lanes] - sine[top, lanes]) * (1.0 / N))
                tendency = []
                for toward_east, toward_north in ((0, 1), (1, 2), (3, 4)):
                    tendency.append(wave_rows * imag[toward_east] + wave_columns * imag[toward_north])
                    tendency.append(
                        -(wave_rows * real[toward_east] + wave_columns * real[toward_north])
                    )
                own = slice(LANES * group, LANES * (group + 1))
                sine_term = terms_ref[2 * phase, :, own]
                cosine_term = terms_ref[2 * phase + 1, :, own]
                result = wave_exponential(
                    tendency, wave_rows, wave_columns, -sine_term, cosine_term
                )
                result = [weight * plane for plane in result]
                total = result if total is None else [a + b for a, b in zip(total, result)]
            main = swap_blocks(total[:4], 32)
            rest = swap_blocks([total[4][:8], total[5][:8], total[4][8:], total[5][8:]], 32)
            for offset in range(4):
                message = jnp.concatenate([main[offset], rest[offset]], axis=0)
                out_ref[slot(4 * group + offset)] = message.astype(BF16)


def last_kernel(state_ref, parts_ref, out_ref):
    mains, rests = [], []
    for part in range(4):
        total = parts_ref[slot(part)].astype(F32)
        for block in range(1, 8):
            total = total + parts_ref[slot(4 * block + part)].astype(F32)
        mains.append(total[:16])
        rests.append(jnp.concatenate([total[16:], roll(total[16:], 64)], axis=0))
    turned = jnp.concatenate(mains + rests, axis=0).T
    row_start = (own_block() * 4 + lax.axis_index("zm") * 2 + lax.axis_index("yh")) * ROWS
    column_start = (lax.axis_index("xy") * 2 + lax.axis_index("c")) * 64
    wave_rows = wave_of(lax.broadcasted_iota(jnp.int32, (ROWS, 64), 0) + row_start)
    wave_columns = wave_of(lax.broadcasted_iota(jnp.int32, (ROWS, 64), 1) + column_start)
    fields = []
    for plane in range(6):
        rows = slice(ROWS * (plane % 4), ROWS * (plane % 4 + 1))
        total = turned[rows, :64] if plane < 4 else turned[rows, 64:]
        fields.append(state_ref[plane // 2, plane % 2] + time_step * total)
    terms = exponential_terms(wave_rows, wave_columns, time_step)
    result = wave_exponential(fields, wave_rows, wave_columns, *terms)
    for plane in range(6):
        out_ref[plane // 2, plane % 2] = result[plane]


def call(kernel, name, shape, dtype, scratch, places, flops, extra=None):
    spots = [pl.BlockSpec(memory_space=pltpu.SMEM if p == "s" else pltpu.VMEM) for p in places]
    whole = pl.BlockSpec(memory_space=pltpu.VMEM)
    shapes = jax.ShapeDtypeStruct(shape, dtype)
    return pl.pallas_call(
        kernel,
        name=name,
        out_shape=(shapes, jax.ShapeDtypeStruct(extra, F32)) if extra else shapes,
        in_specs=spots,
        out_specs=(whole, whole) if extra else whole,
        scratch_shapes=[pltpu.VMEM(s, BF16) for s in scratch],
        cost_estimate=pl.CostEstimate(flops=flops, bytes_accessed=1 << 20, transcendentals=0),
        compiler_params=pltpu.CompilerParams(vmem_limit_bytes=VMEM_LIMIT),
    )


def per_device(spectral_state, phase_index, weight_count):
    tables, turned_tables = fourier_tables()
    spread = call(spread_kernel, "spread", (32, 24, LANES), BF16, [], "v", 1 << 33)(spectral_state)
    settings = call(settings_kernel, "settings", (8, LANES), F32, [], "ss", 1 << 12)(
        phase_index, weight_count
    )
    settings = lax.all_gather(settings, "c")
    settings = lax.ppermute(
        settings, ("xy", "zh", "zl"), [(8 * i + j, 8 * j + i) for i in range(8) for j in range(8)]
    )
    gathered = lax.all_to_all(spread, MAIN_AXES, 0, 0)
    outgoing, terms = call(first_kernel, "inverse_rows", (64, 24, LANES), BF16, [(384, N)], "vvv", 1 << 30, (4, LINES, N))(
        settings, gathered, tables
    )
    arrived = lax.all_to_all(outgoing, GROUP_AXES, 0, 0)
    outgoing_back = call(
        second_kernel,
        "grid_products",
        (64, 40, LANES),
        BF16,
        [(N, 2 * LANES), (N, 2 * LANES), (N, 4 * LANES)],
        "vv",
        1 << 30,
    )(arrived, turned_tables)
    returned = lax.all_to_all(outgoing_back, GROUP_AXES, 0, 0)
    weighted = call(third_kernel, "forward_rows", (32, 24, LANES), BF16, [(640, N)], "vvvv", 1 << 31)(
        settings, terms, returned, tables
    )
    parts = lax.all_to_all(weighted, MAIN_AXES, 0, 0)
    return call(last_kernel, "advance", spectral_state.shape, F32, [], "vv", 1 << 24)(spectral_state, parts)


def solution(mesh):
    fine = Mesh(mesh.devices.reshape(8, 2, 2, 4, 2, 2), ("xy", "c", "zh", "zl", "zm", "yh"))
    rows, columns = ("zh", "zl", "zm", "yh"), ("xy", "c")
    in_specs = (P(None, None, rows, columns), P(columns), P(columns))
    out_specs = P(None, None, rows, columns)
    return jax.shard_map(
        per_device, mesh=fine, in_specs=in_specs, out_specs=out_specs, check_vma=False
    )
```
